32 devices in a mesh: grp: 2 (over y), dp: 8 (over z, x), mp: 2 (over core).
Axes of the slice: x: 2, y: 2, z: 4, core: 2. Of those that a mesh axis runs over, the one named last changes fastest.
Arguments:
- cand_x: bfloat16 [384, 16, 5120], P(('grp', 'dp')), parts along dimension 0
- val_x: bfloat16 [256, 16, 5120], P(('grp', 'dp')), parts along dimension 0
- cand_grad: bfloat16 [384, 16, 5120], P(('grp', 'dp')), parts along dimension 0
- val_grad: bfloat16 [256, 16, 5120], P(('grp', 'dp')), parts along dimension 0
- cand_attn: bfloat16 [384, 16, 5120], P(('grp', 'dp'), None, 'mp'), parts along dimension 0
- val_attn: bfloat16 [256, 16, 5120], P(('grp', 'dp'), None, 'mp'), parts along dimension 0
- cand_probs: bfloat16 [384, 40, 16, 16], P(('grp', 'dp'), 'mp'), parts along dimension 0, as said below
- val_probs: bfloat16 [256, 40, 16, 16], P(('grp', 'dp'), 'mp'), parts along dimension 0, as said below
- cand_len: int32 [384], P(('grp', 'dp')), parts along dimension 0, may hold values from 4 to 16, as said below
- val_len: int32 [256], P(('grp', 'dp')), parts along dimension 0, may hold values from 4 to 16, as said below
- out_weight: bfloat16 [5120, 5120], P('mp', 'dp'), may hold values from -0.078125 to 0.078125
- input_proj: bfloat16 [5120, 64], replicated, may hold values from -0.078125 to 0.078125
- grad_proj: bfloat16 [5120, 128], replicated, may hold values from -0.078125 to 0.078125
- attn_proj: bfloat16 [5120, 64], P('mp'), may hold values from -0.078125 to 0.078125
- value_proj: bfloat16 [1024, 128], P('mp'), may hold values from -0.1875 to 0.1875
Outputs:
- scores: float32 [384, 128], P(('grp', 'dp')), parts along dimension 0
The draws below stay inside these ranges and needn't reach their ends.
There are 2 independent parts, one for each index of `grp`. The reference program is written for one: setup_inputs(seed, part) draws one part's arguments, and reference() takes and returns one part's arrays. A program takes and returns all parts, laid end to end along the dimension named above; an argument that names none is the same for every part. Nothing has to cross between parts.
Inputs may be any that keep to these rules, and one draw needn't show every extreme that they name: `cand_len`: each prompt has at least 4 live tokens; some prompt of each set is full. `val_len`: each prompt has at least 4 live tokens; some prompt of each set is full. `cand_probs`: Causal: entries with key after query are zero; each query row sums to one up to rounding. `val_probs`: Causal: entries with key after query are zero; each query row sums to one up to rounding.
All inputs are finite; a program needn't handle non-finite values.
Results may differ from the reference program's by a relative error of at most 0.0022.
Values may be sent and summed in bfloat16 or wider, within the bound.
A program may use at most 192 MiB of HBM per device.

```python
import jax
import jax.numpy as jnp
from jax import lax

D = 5120
HEADS = 40
KV_HEADS = 8
HEAD_DIM = 128
KA = 64
KB = 128
SEQ = 16
KV_DIM = 1024
CAND = 192
VAL = 128


def template(key, salt):
    return jax.random.normal(jax.random.fold_in(key, salt), (SEQ, D), jnp.float32)


def mixed_rows(key, count, shared, noise_weight):
    noise_key = jax.random.fold_in(key, 0)
    noise = jax.random.normal(noise_key, (count, SEQ, D), jnp.float32)
    return (0.8 * shared[None] + noise_weight * noise).astype(jnp.bfloat16)


def causal_probs(key, count, reach):
    logits = jax.random.uniform(key, (count, HEADS, SEQ, SEQ), jnp.float32, -reach, reach)
    query = jnp.arange(SEQ)[:, None]
    keyed = jnp.arange(SEQ)[None, :]
    weights = jnp.exp(logits) * (keyed <= query).astype(jnp.float32)
    return (weights / jnp.sum(weights, axis=-1, keepdims=True)).astype(jnp.bfloat16)


def prompt_lengths(key, count):
    first, second = jax.random.split(key)
    length = jax.random.randint(first, (count,), SEQ // 4, SEQ + 1)
    full = jax.random.randint(second, (), 0, count)
    return length.at[full].set(SEQ).astype(jnp.int32)


def draw_cand_x(key, part):
    shared = template(key, 101)
    key = jax.random.fold_in(key, 1)
    return mixed_rows(key, CAND, shared, 0.6)


def draw_val_x(key, part):
    shared = template(key, 101)
    key = jax.random.fold_in(key, 2)
    return mixed_rows(key, VAL, shared, 0.6)


def draw_cand_grad(key, part):
    shared = template(key, 102)
    key = jax.random.fold_in(key, 3)
    return mixed_rows(key, CAND, shared, 0.6)


def draw_val_grad(key, part):
    shared = template(key, 102)
    key = jax.random.fold_in(key, 4)
    return mixed_rows(key, VAL, shared, 0.6)


def draw_cand_attn(key, part):
    shared = template(key, 103)
    key = jax.random.fold_in(key, 5)
    return mixed_rows(key, CAND, shared, 0.6)


def draw_val_attn(key, part):
    shared = template(key, 103)
    key = jax.random.fold_in(key, 6)
    return mixed_rows(key, VAL, shared, 0.6)


def draw_cand_probs(key, part):
    key = jax.random.fold_in(key, 7)
    return causal_probs(key, CAND, 2.0)


def draw_val_probs(key, part):
    key = jax.random.fold_in(key, 8)
    return causal_probs(key, VAL, 2.0)


def draw_cand_len(key, part):
    key = jax.random.fold_in(key, 9)
    return prompt_lengths(key, CAND)


def draw_val_len(key, part):
    key = jax.random.fold_in(key, 10)
    return prompt_lengths(key, VAL)


def shard_levels(stream_key, shape, cuts, smallest, largest):
    level, own = 1.0, jax.random.fold_in(stream_key, 6)
    for position, blocks in cuts:
        steps = jnp.exp(jax.random.uniform(jax.random.fold_in(own, position), (blocks,), jnp.float32, smallest / len(cuts), largest / len(cuts)))
        level = level * jnp.repeat(steps, shape[position] // blocks).reshape([-1 if axis == position else 1 for axis in range(len(shape))])
    return level


def scatter_about(rng, extent, scale, bound, shards=(), kind=jnp.bfloat16):
    values = jax.random.normal(rng, extent, jnp.float32) * scale
    if len(shards) > 0:
        values = shard_levels(rng, extent, shards, -0.22, 0.18) * values
    return jnp.clip(values, min=-bound, max=bound).astype(kind)


def setup_inputs(seed: int = 0, part: int = 0) -> dict:
    splits = jax.random.split(jax.random.key(seed), 16)
    part_keys = jax.random.split(jax.random.fold_in(splits[15], part), 16)
    cand_x = draw_cand_x(jax.random.fold_in(jax.random.fold_in(splits[15], part), 71), part)
    val_x = draw_val_x(jax.random.fold_in(jax.random.fold_in(splits[15], part), 71), part)
    cand_grad = draw_cand_grad(jax.random.fold_in(jax.random.fold_in(splits[15], part), 71), part)
    val_grad = draw_val_grad(jax.random.fold_in(jax.random.fold_in(splits[15], part), 71), part)
    cand_attn = draw_cand_attn(jax.random.fold_in(jax.random.fold_in(splits[15], part), 71), part)
    val_attn = draw_val_attn(jax.random.fold_in(jax.random.fold_in(splits[15], part), 71), part)
    cand_probs = draw_cand_probs(jax.random.fold_in(jax.random.fold_in(splits[15], part), 71), part)
    val_probs = draw_val_probs(jax.random.fold_in(jax.random.fold_in(splits[15], part), 71), part)
    cand_len = draw_cand_len(jax.random.fold_in(jax.random.fold_in(splits[15], part), 71), part)
    val_len = draw_val_len(jax.random.fold_in(jax.random.fold_in(splits[15], part), 71), part)
    out_weight = scatter_about(splits[10], (D, D), D ** -0.5, 0.078125, ((0, 2), (1, 8)))
    input_proj = scatter_about(splits[11], (D, KA), D ** -0.5, 0.078125)
    grad_proj = scatter_about(splits[12], (D, KB), D ** -0.5, 0.078125)
    attn_proj = scatter_about(splits[13], (D, KA), D ** -0.5, 0.078125, ((0, 2),))
    value_proj = scatter_about(splits[14], (KV_DIM, KB), KV_DIM ** -0.5, 0.1875, ((0, 2),))
    return {"cand_x": cand_x, "val_x": val_x, "cand_grad": cand_grad, "val_grad": val_grad, "cand_attn": cand_attn, "val_attn": val_attn, "cand_probs": cand_probs, "val_probs": val_probs, "cand_len": cand_len, "val_len": val_len, "out_weight": out_weight, "input_proj": input_proj, "grad_proj": grad_proj, "attn_proj": attn_proj, "value_proj": value_proj}


def prompt_features(x, grad, attn, probs, length, out_weight, input_proj, grad_proj, attn_proj, value_proj):
    count = x.shape[0]
    positions = jnp.arange(SEQ, dtype=jnp.int32)
    mask = (positions[None, :] < length[:, None]).astype(jnp.bfloat16)
    masked = grad * mask[:, :, None]
    flat_grad = masked.reshape(count * SEQ, D)
    grad_attn = jnp.dot(flat_grad, out_weight.T, preferred_element_type=jnp.float32).astype(jnp.bfloat16)
    grad_heads = grad_attn.reshape(count, SEQ, HEADS, HEAD_DIM).astype(jnp.float32)
    mixed = jnp.einsum('ehij,eihd->ejhd', probs.astype(jnp.float32), grad_heads)
    group = HEADS // KV_HEADS
    grad_value = lax.optimization_barrier(jnp.sum(mixed.reshape(count, SEQ, KV_HEADS, group, HEAD_DIM), axis=3))
    grad_value = grad_value.reshape(count * SEQ, KV_DIM).astype(jnp.bfloat16)
    a_in = jnp.dot(x.reshape(count * SEQ, D), input_proj, preferred_element_type=jnp.float32).reshape(count, SEQ, KA)
    b_val = jnp.dot(grad_value, value_proj, preferred_element_type=jnp.float32).reshape(count, SEQ, KB)
    a_att = jnp.dot(attn.reshape(count * SEQ, D), attn_proj, preferred_element_type=jnp.float32).reshape(count, SEQ, KA)
    b_out = jnp.dot(flat_grad, grad_proj, preferred_element_type=jnp.float32).reshape(count, SEQ, KB)
    feat_out = jnp.einsum('eta,etb->eab', a_att, b_out).reshape(count, KA * KB)
    feat_val = jnp.einsum('eta,etb->eab', a_in, b_val).reshape(count, KA * KB)
    feat = jnp.concatenate([feat_out, feat_val], axis=1)
    total = lax.optimization_barrier(jnp.sum(feat * feat, axis=1, keepdims=True))
    return (feat * lax.rsqrt(total + 1e-06)).astype(jnp.bfloat16)

def reference(cand_x, val_x, cand_grad, val_grad, cand_attn, val_attn, cand_probs, val_probs, cand_len, val_len, out_weight, input_proj, grad_proj, attn_proj, value_proj):
    unit_cand = prompt_features(cand_x, cand_grad, cand_attn, cand_probs, cand_len, out_weight, input_proj, grad_proj, attn_proj, value_proj)
    unit_val = prompt_features(val_x, val_grad, val_attn, val_probs, val_len, out_weight, input_proj, grad_proj, attn_proj, value_proj)
    return jnp.dot(unit_cand, unit_val.T, preferred_element_type=jnp.float32)
```

```python
import jax
import jax.numpy as jnp
from jax import lax
from jax.sharding import PartitionSpec as P

HEAD_DIM = 128
EPS = 1e-06


def dot(left, right, contract):
    return lax.dot_general(
        left, right, ((contract[:1], contract[1:]), ((), ())), preferred_element_type=jnp.float32
    )


def gram(left_a, left_b, right_a, right_b):
    return dot(left_a, right_a, (1, 1)) * dot(left_b, right_b, (1, 1))


def own(cand, val, n_mp, index):
    cand_rows, val_rows = cand.shape[0] // n_mp, val.shape[0] // n_mp
    return jnp.concatenate(
        [
            lax.dynamic_slice_in_dim(cand, index * cand_rows, cand_rows, 0),
            lax.dynamic_slice_in_dim(val, index * val_rows, val_rows, 0),
        ],
        axis=0,
    )


def regroup(cand, val, n_mp):
    cand = cand.reshape((n_mp, cand.shape[0] // n_mp) + cand.shape[1:])
    val = val.reshape((n_mp, val.shape[0] // n_mp) + val.shape[1:])
    both = jnp.concatenate([cand, val], axis=1)
    return both.reshape((both.shape[0] * both.shape[1],) + both.shape[2:])


def folded(out_weight, value_proj, local_heads):
    local_kv = value_proj.shape[0] // HEAD_DIM
    group = local_heads // local_kv
    weight = out_weight.reshape(local_kv, group, HEAD_DIM, out_weight.shape[1])
    proj = value_proj.reshape(local_kv, HEAD_DIM, value_proj.shape[1])
    fold = jnp.einsum("kgdf,kdb->fkgb", weight, proj, preferred_element_type=jnp.float32)
    return fold.reshape(out_weight.shape[1], local_heads, -1).astype(jnp.bfloat16)


def local(n_mp, cand_x, val_x, cand_grad, val_grad, cand_attn, val_attn, cand_probs, val_probs,
          cand_len, val_len, out_weight, input_proj, grad_proj, attn_proj, value_proj):
    index = lax.axis_index("mp")
    seq, width = cand_x.shape[1:]
    n_cand = cand_x.shape[0] // n_mp
    count = n_cand + val_x.shape[0] // n_mp
    tokens = count * seq
    heads = cand_probs.shape[1]
    features = out_weight.shape[1]
    n_dp = width // features
    positions = jnp.arange(seq, dtype=jnp.int32)

    grads = own(cand_grad, val_grad, n_mp, index).reshape(tokens, width)
    inputs = own(cand_x, val_x, n_mp, index).reshape(tokens, width)
    length = regroup(cand_len, val_len, n_mp)
    probs = regroup(cand_probs, val_probs, n_mp)
    mask = positions[None, :] < length[:, None]
    probs = jnp.where(mask[:, None, :, None], probs, 0)
    probs = probs.transpose(0, 3, 1, 2).reshape(n_mp * tokens, heads, seq)
    probs = lax.all_to_all(probs, "mp", 0, 1, tiled=True)
    attn = regroup(cand_attn, val_attn, n_mp).reshape(n_mp * tokens, -1)

    spread = lax.all_to_all(grads.reshape(tokens, n_dp, features), "dp", 1, 0, tiled=True)
    spread = spread.reshape(n_dp * count * seq, features)
    probs = lax.all_gather(probs, "dp", axis=0, tiled=True)
    fold = lax.all_gather(folded(out_weight, value_proj, heads), "mp", axis=1, tiled=True)
    all_heads = heads * n_mp
    mixed = dot(spread, fold.reshape(features, -1), (1, 0)).astype(jnp.bfloat16)
    mixed = mixed.reshape(n_dp * count, seq, all_heads, -1)
    probs = probs.reshape(n_dp * count, seq, all_heads, seq)
    b_val = jnp.einsum("ejhi,eihb->ejb", probs, mixed, preferred_element_type=jnp.float32)
    b_val = lax.psum_scatter(b_val, "dp", scatter_dimension=0, tiled=True).reshape(tokens, -1)

    a_in = dot(inputs, input_proj, (1, 0)).astype(jnp.bfloat16)
    live = (positions[None, :] < own(cand_len, val_len, n_mp, index)[:, None]).reshape(tokens, 1)
    b_out = jnp.where(live, dot(grads, grad_proj, (1, 0)), 0.0)
    a_att = dot(attn, attn_proj, (1, 0))
    a_att = lax.psum_scatter(a_att, "mp", scatter_dimension=0, tiled=True).astype(jnp.bfloat16)

    low_out, low_val = b_out.astype(jnp.bfloat16), b_val.astype(jnp.bfloat16)
    square = gram(a_att, low_out, a_att, low_out) + gram(a_in, low_val, a_in, low_val)
    which = jnp.arange(tokens) // seq
    total = jnp.sum(jnp.where(which[:, None] == which[None, :], square, 0.0), axis=1)
    total = jnp.sum(total.reshape(count, seq), axis=1)
    scale = jnp.repeat(lax.rsqrt(jnp.maximum(total, 0.0) + EPS), seq)[:, None]
    factors = jnp.concatenate(
        [a_att, a_in, (b_out * scale).astype(jnp.bfloat16), (b_val * scale).astype(jnp.bfloat16)], axis=1
    )
    rows = n_cand * seq
    ours = factors[:rows]
    theirs = lax.all_gather(factors[rows:], ("dp", "mp"), axis=0, tiled=True)
    ka, kb = a_in.shape[1], b_out.shape[1]
    cuts = (slice(0, ka), slice(2 * ka, 2 * ka + kb), slice(ka, 2 * ka), slice(2 * ka + kb, None))
    first, second, third, fourth = [(ours[:, cut], theirs[:, cut]) for cut in cuts]
    product = gram(first[0], second[0], first[1], second[1]) + gram(third[0], fourth[0], third[1], fourth[1])
    scores = jnp.sum(product.reshape(n_cand, seq, -1, seq), axis=(1, 3))
    return lax.all_gather(scores, "mp", axis=0, tiled=True)


def solution(mesh):
    placed = (
        P(("grp", "dp"), None, None),
        P(("grp", "dp"), None, None),
        P(("grp", "dp"), None, None),
        P(("grp", "dp"), None, None),
        P(("grp", "dp"), None, "mp"),
        P(("grp", "dp"), None, "mp"),
        P(("grp", "dp"), "mp", None, None),
        P(("grp", "dp"), "mp", None, None),
        P(("grp", "dp")),
        P(("grp", "dp")),
        P("mp", "dp"),
        P(),
        P(),
        P("mp", None),
        P("mp", None),
    )

    def body(*args):
        return local(mesh.shape["mp"], *args)

    return jax.shard_map(
        body, mesh=mesh, in_specs=placed, out_specs=P(("grp", "dp"), None), check_vma=False
    )
```

```python
import functools

import jax
import jax.numpy as jnp
from jax import lax
from jax.experimental import pallas as pl
from jax.experimental.pallas import tpu as pltpu
from jax.sharding import PartitionSpec as P

HEAD_DIM = 128
EPS = 1e-06


def dot(left, right, contract):
    return lax.dot_general(
        left, right, ((contract[:1], contract[1:]), ((), ())), preferred_element_type=jnp.float32
    )


def gram(left_a, left_b, right_a, right_b):
    return dot(left_a, right_a, (1, 1)) * dot(left_b, right_b, (1, 1))


def own(cand, val, n_mp, index):
    cand_rows, val_rows = cand.shape[0] // n_mp, val.shape[0] // n_mp
    return jnp.concatenate(
        [
            lax.dynamic_slice_in_dim(cand, index * cand_rows, cand_rows, 0),
            lax.dynamic_slice_in_dim(val, index * val_rows, val_rows, 0),
        ],
        axis=0,
    )


def regroup(cand, val, n_mp):
    cand = cand.reshape((n_mp, cand.shape[0] // n_mp) + cand.shape[1:])
    val = val.reshape((n_mp, val.shape[0] // n_mp) + val.shape[1:])
    both = jnp.concatenate([cand, val], axis=1)
    return both.reshape((both.shape[0] * both.shape[1],) + both.shape[2:])


def folded(out_weight, value_proj, local_heads):
    local_kv = value_proj.shape[0] // HEAD_DIM
    group = local_heads // local_kv
    weight = out_weight.reshape(local_kv, group, HEAD_DIM, out_weight.shape[1])
    proj = value_proj.reshape(local_kv, HEAD_DIM, value_proj.shape[1])
    fold = jnp.einsum("kgdf,kdb->fkgb", weight, proj, preferred_element_type=jnp.float32)
    return fold.reshape(out_weight.shape[1], local_heads, -1).astype(jnp.bfloat16)


def local(n_mp, cand_x, val_x, cand_grad, val_grad, cand_attn, val_attn, cand_probs, val_probs,
          cand_len, val_len, out_weight, input_proj, grad_proj, attn_proj, value_proj):
    index = lax.axis_index("mp")
    seq, width = cand_x.shape[1:]
    n_cand = cand_x.shape[0] // n_mp
    count = n_cand + val_x.shape[0] // n_mp
    tokens = count * seq
    heads = cand_probs.shape[1]
    features = out_weight.shape[1]
    n_dp = width // features
    positions = jnp.arange(seq, dtype=jnp.int32)

    grads = own(cand_grad, val_grad, n_mp, index).reshape(tokens, width)
    inputs = own(cand_x, val_x, n_mp, index).reshape(tokens, width)
    length = regroup(cand_len, val_len, n_mp)
    probs = regroup(cand_probs, val_probs, n_mp)
    mask = positions[None, :] < length[:, None]
    probs = jnp.where(mask[:, None, :, None], probs, 0)
    probs = probs.transpose(0, 3, 1, 2).reshape(n_mp * tokens, heads, seq)
    probs = lax.all_to_all(probs, "mp", 0, 1, tiled=True)
    attn = regroup(cand_attn, val_attn, n_mp).reshape(n_mp * tokens, -1)

    spread = lax.all_to_all(grads.reshape(tokens, n_dp, features), "dp", 1, 0, tiled=True)
    spread = spread.reshape(n_dp * count * seq, features)
    probs = lax.all_gather(probs, "dp", axis=0, tiled=True)
    fold = lax.all_gather(folded(out_weight, value_proj, heads), "mp", axis=1, tiled=True)
    all_heads = heads * n_mp
    mixed = dot(spread, fold.reshape(features, -1), (1, 0)).astype(jnp.bfloat16)
    mixed = mixed.reshape(n_dp * count, seq, all_heads, -1)
    probs = probs.reshape(n_dp * count, seq, all_heads, seq)
    b_val = jnp.einsum("ejhi,eihb->ejb", probs, mixed, preferred_element_type=jnp.float32)
    b_val = lax.psum_scatter(b_val, "dp", scatter_dimension=0, tiled=True).reshape(tokens, -1)

    a_in = dot(inputs, input_proj, (1, 0)).astype(jnp.bfloat16)
    live = (positions[None, :] < own(cand_len, val_len, n_mp, index)[:, None]).reshape(tokens, 1)
    b_out = jnp.where(live, dot(grads, grad_proj, (1, 0)), 0.0)
    a_att = dot(attn, attn_proj, (1, 0))
    a_att = lax.psum_scatter(a_att, "mp", scatter_dimension=0, tiled=True).astype(jnp.bfloat16)

    low_out, low_val = b_out.astype(jnp.bfloat16), b_val.astype(jnp.bfloat16)
    square = gram(a_att, low_out, a_att, low_out) + gram(a_in, low_val, a_in, low_val)
    which = jnp.arange(tokens) // seq
    total = jnp.sum(jnp.where(which[:, None] == which[None, :], square, 0.0), axis=1)
    total = jnp.sum(total.reshape(count, seq), axis=1)
    scale = jnp.repeat(lax.rsqrt(jnp.maximum(total, 0.0) + EPS), seq)[:, None]
    factors = jnp.concatenate(
        [a_att, a_in, (b_out * scale).astype(jnp.bfloat16), (b_val * scale).astype(jnp.bfloat16)], axis=1
    )
    rows = n_cand * seq
    ours = factors[:rows]
    theirs = lax.all_gather(factors[rows:], ("dp", "mp"), axis=0, tiled=True)
    ka, kb = a_in.shape[1], b_out.shape[1]
    cuts = (slice(0, ka), slice(2 * ka, 2 * ka + kb), slice(ka, 2 * ka), slice(2 * ka + kb, None))
    first, second, third, fourth = [(ours[:, cut], theirs[:, cut]) for cut in cuts]
    product = gram(first[0], second[0], first[1], second[1]) + gram(third[0], fourth[0], third[1], fourth[1])
    scores = jnp.sum(product.reshape(n_cand, seq, -1, seq), axis=(1, 3))
    return lax.all_gather(scores, "mp", axis=0, tiled=True)


def remote(src, dst, send_sem, recv_sem, device_id):
    return pltpu.make_async_remote_copy(
        src_ref=src, dst_ref=dst, send_sem=send_sem, recv_sem=recv_sem,
        device_id=device_id, device_id_type=pl.DeviceIdType.MESH,
    )


def kernel(
    n_dp,
    cand_len, val_len, cand_x, val_x, cand_grad, val_grad, cand_attn, val_attn, cand_probs, val_probs,
    out_weight, input_proj, grad_proj, attn_proj, value_proj,
    scores,
    g_own, x_own, attn, c_probs, v_probs, weight, g_all, x_half, x_other, x_all, fold, mixed,
    att_send, att_recv, b_own, b_send, b_recv, factor_own, factor_sib, factor_val, out_own, out_sib,
    load_sem, g_send, g_recv, x_send, x_recv, hop_send, fold_send, fold_recv, bs_send, bs_recv,
    f_send, f_recv, pair_send, pair_recv,
):
    dp, mp = lax.axis_index("dp"), lax.axis_index("mp")
    sibling = {"mp": 1 - mp}
    seq = c_probs.shape[2]
    n_cand, n_val = c_probs.shape[0] // 2, v_probs.shape[0] // 2
    count = n_cand + n_val
    rows_c, rows_v = n_cand * seq, n_val * seq
    tokens = rows_c + rows_v
    features = weight.shape[1]
    local_heads = c_probs.shape[1]
    local_kv = value_proj.shape[0] // HEAD_DIM
    group = local_heads // local_kv
    kb = value_proj.shape[1]
    ka = input_proj.shape[1]

    barrier = pltpu.get_barrier_semaphore()
    for step in range(1, n_dp):
        pl.semaphore_signal(barrier, inc=1, device_id={"dp": lax.rem(dp + step, n_dp)}, device_id_type=pl.DeviceIdType.MESH)
    pl.semaphore_signal(barrier, inc=1, device_id=sibling, device_id_type=pl.DeviceIdType.MESH)

    own_c = pl.ds(pl.multiple_of(mp * rows_c, 16), rows_c)
    own_v = pl.ds(pl.multiple_of(mp * rows_v, 16), rows_v)
    mine = pl.ds(pl.multiple_of(dp * features, 128), features)
    all_c = cand_attn.shape[0]
    loads = []
    pairs = (
        (cand_probs, c_probs), (val_probs, v_probs), (out_weight, weight),
        (cand_grad.at[own_c], g_own.at[pl.ds(0, rows_c)]), (val_grad.at[own_v], g_own.at[pl.ds(rows_c, rows_v)]),
        (cand_attn, attn.at[pl.ds(0, all_c)]), (val_attn, attn.at[pl.ds(all_c, val_attn.shape[0])]),
        (cand_x.at[own_c], x_own.at[pl.ds(0, rows_c)]), (val_x.at[own_v], x_own.at[pl.ds(rows_c, rows_v)]),
        (cand_grad.at[own_c, mine], g_all.at[dp, pl.ds(0, rows_c)]),
        (val_grad.at[own_v, mine], g_all.at[dp, pl.ds(rows_c, rows_v)]),
    )
    for slot, (src, dst) in enumerate(pairs):
        load = pltpu.make_async_copy(src, dst, load_sem.at[slot])
        load.start()
        loads.append(load)
    pl.semaphore_wait(barrier, n_dp)

    g_copies = []
    for step in range(1, n_dp):
        peer = lax.rem(dp + step, n_dp)
        theirs = pl.ds(pl.multiple_of(peer * features, 128), features)
        for part, (src, rows, at) in enumerate(((cand_grad, own_c, pl.ds(0, rows_c)), (val_grad, own_v, pl.ds(rows_c, rows_v)))):
            copy = remote(src.at[rows, theirs], g_all.at[dp, at], g_send.at[part, peer], g_recv.at[part, dp], {"dp": peer})
            copy.start()
            g_copies.append(copy)

    loads[0].wait()
    loads[1].wait()
    width = local_heads * seq
    eye = (lax.broadcasted_iota(jnp.int32, (seq, seq), 0) == lax.broadcasted_iota(jnp.int32, (seq, seq), 1)).astype(jnp.bfloat16)
    query = lax.rem(lax.broadcasted_iota(jnp.int32, (seq, width), 1), seq)

    def turn(source, lengths, per_half, offset):
        def body(e, carry):
            flat = source[e].reshape(width, seq)
            turned = dot(eye, flat, (1, 1))
            turned = jnp.where(query < lengths[e], turned, 0.0).astype(jnp.bfloat16)
            at = pl.multiple_of((offset + lax.rem(e, per_half)) * seq, 16)
            x_half[lax.div(e, per_half), pl.ds(at, seq), :] = turned
            return carry
        lax.fori_loop(0, 2 * per_half, body, 0)

    turn(c_probs, cand_len, n_cand, 0)
    turn(v_probs, val_len, n_val, n_cand)
    x_pair = remote(x_half.at[1 - mp], x_other, pair_send.at[0], pair_recv.at[0], sibling)
    x_pair.start()

    loads[2].wait()
    fold_copies = []
    for k in range(local_kv):
        proj = value_proj[k * HEAD_DIM:(k + 1) * HEAD_DIM, :].T
        for h in range(group):
            at = (k * group + h) * HEAD_DIM
            rows = pl.ds(pl.multiple_of((mp * local_heads + k * group + h) * kb, 128), kb)
            fold[rows, :] = dot(proj, weight[at:at + HEAD_DIM, :], (1, 0)).astype(jnp.bfloat16)
        span = pl.ds(pl.multiple_of((mp * local_heads + k * group) * kb, 128), group * kb)
        copy = remote(fold.at[span], fold.at[span], fold_send.at[k], fold_recv.at[k], sibling)
        copy.start()
        fold_copies.append(copy)
        if k == 0:
            x_pair.wait()
            first, other = x_half[mp], x_other[...]
            low, high = jnp.where(mp == 0, first, other), jnp.where(mp == 0, other, first)
            x_all[dp] = jnp.concatenate([low, high], axis=1)
            partner = {"dp": dp + 1 - 2 * lax.rem(dp, 2)}
            x_copies = []
            for step in range(2, n_dp, 2):
                peer = lax.rem(dp + step, n_dp)
                copy = remote(x_all.at[dp], x_all.at[dp], x_send.at[peer], x_recv.at[dp], {"dp": peer})
                copy.start()
                x_copies.append(copy)
            copy = remote(x_all.at[dp], x_all.at[dp], hop_send.at[dp], x_recv.at[dp], partner)
            copy.start()
            x_copies.append(copy)

    loads[5].wait()
    loads[6].wait()
    for half in range(2):
        att_send[half, pl.ds(0, rows_c), :] = dot(attn[half * rows_c:(half + 1) * rows_c, :], attn_proj[...], (1, 0))
        att_send[half, pl.ds(rows_c, rows_v), :] = dot(
            attn[all_c + half * rows_v:all_c + (half + 1) * rows_v, :], attn_proj[...], (1, 0))
    att_pair = remote(att_send.at[1 - mp], att_recv, pair_send.at[1], pair_recv.at[1], sibling)
    att_pair.start()
    for slot in (3, 4, 7, 8, 9, 10):
        loads[slot].wait()
    a_in = dot(x_own[...], input_proj[...], (1, 0)).astype(jnp.bfloat16)
    b_own[...] = dot(g_own[...], grad_proj[...], (1, 0))
    position = lax.broadcasted_iota(jnp.int32, (seq, kb), 0)
    for e in range(count):
        live = cand_len[mp * n_cand + e] if e < n_cand else val_len[mp * n_val + e - n_cand]
        at = slice(e * seq, (e + 1) * seq)
        b_own[at, :] = jnp.where(position < live, b_own[at, :], 0.0)
    att_pair.wait()
    a_att = (att_send[mp] + att_recv[...]).astype(jnp.bfloat16)
    factor_own[:, 0:2 * ka] = jnp.concatenate([a_att, a_in], axis=1)

    for step in range(2, n_dp, 2):
        source = lax.rem(dp - step + n_dp, n_dp)
        remote(x_all.at[source], x_all.at[source], x_send.at[source], x_recv.at[source], partner).wait_recv()
        copy = remote(x_all.at[source], x_all.at[source], hop_send.at[source], x_recv.at[source], partner)
        copy.start()
        x_copies.append(copy)
    for k in range(local_kv):
        span = pl.ds(pl.multiple_of(((1 - mp) * local_heads + k * group) * kb, 128), group * kb)
        remote(fold.at[span], fold.at[span], fold_send.at[k], fold_recv.at[k], sibling).wait_recv()

    heads = 2 * local_heads
    batch = 4

    def block(source):
        def heads_step(c, carry):
            rows = pl.ds(pl.multiple_of(c * batch * kb, 128), batch * kb)
            part = dot(g_all[source], fold[rows, :], (1, 1)).astype(jnp.bfloat16)
            for h in range(batch):
                at = pl.ds(pl.multiple_of((c * batch + h) * seq, 16), seq)
                mixed[:, at, :] = part[:, h * kb:(h + 1) * kb].reshape(count, seq, kb)
            return carry
        lax.fori_loop(0, heads // batch, heads_step, 0)

        def prompt_step(e, carry):
            at = pl.ds(pl.multiple_of(e * seq, 16), seq)
            b_send[source, at, :] = dot(x_all[source, at, :], mixed[e], (1, 0)).astype(jnp.bfloat16)
            return carry
        lax.fori_loop(0, count, prompt_step, 0, unroll=4)

    block(dp)
    b_val = b_send[dp].astype(jnp.float32)

    order = range(1, n_dp)

    def receive(step, waited):
        source = lax.rem(dp - step + n_dp, n_dp)
        for part, at in enumerate((pl.ds(0, rows_c), pl.ds(rows_c, rows_v))):
            remote(g_all.at[source, at], g_all.at[source, at], g_send.at[part, source], g_recv.at[part, source], {"dp": source}).wait_recv()
        if not waited:
            remote(x_all.at[source], x_all.at[source], hop_send.at[source], x_recv.at[source], {"dp": source}).wait_recv()
        block(source)
        copy = remote(b_send.at[source], b_recv.at[dp], bs_send.at[source], bs_recv.at[dp], {"dp": source})
        copy.start()
        return copy

    b_copies = [receive(step, step % 2 == 0) for step in order]
    for step in order:
        source = lax.rem(dp - step + n_dp, n_dp)
        remote(b_recv.at[source], b_recv.at[source], bs_send.at[source], bs_recv.at[source], {"dp": source}).wait_recv()
        b_val = b_val + b_recv[source].astype(jnp.float32)

    low_out, low_val = b_own[...].astype(jnp.bfloat16), b_val.astype(jnp.bfloat16)
    square = gram(a_att, low_out, a_att, low_out) + gram(a_in, low_val, a_in, low_val)
    one = lax.div(lax.broadcasted_iota(jnp.int32, (tokens, tokens), 0), seq)
    two = lax.div(lax.broadcasted_iota(jnp.int32, (tokens, tokens), 1), seq)
    same = one == two
    square = jnp.sum(jnp.where(same, square, 0.0), axis=1, keepdims=True)
    square = jnp.broadcast_to(square, (tokens, 128))
    total = lax.dot_general(same.astype(jnp.float32), square, (((1,), (0,)), ((), ())),
                            precision=lax.Precision.HIGHEST, preferred_element_type=jnp.float32)
    scale = lax.rsqrt(jnp.maximum(total[:, 0:1], 0.0) + EPS)
    factor_own[:, 2 * ka:2 * ka + kb] = (b_own[...] * scale).astype(jnp.bfloat16)
    factor_own[:, 2 * ka + kb:] = (b_val * scale).astype(jnp.bfloat16)
    f_copies = []
    val_rows, cand_rows = pl.ds(rows_c, rows_v), pl.ds(0, rows_c)
    for step in order:
        peer = lax.rem(dp + step, n_dp)
        copy = remote(factor_own.at[val_rows], factor_val.at[dp], f_send.at[peer], f_recv.at[dp], {"dp": peer})
        copy.start()
        f_copies.append(copy)
    f_pair = remote(factor_own.at[cand_rows], factor_sib, pair_send.at[2], pair_recv.at[2], sibling)
    f_pair.start()
    for copy in g_copies + x_copies + fold_copies + b_copies:
        copy.wait_send()
    f_pair.wait()

    first, other = factor_own[0:rows_c, :], factor_sib[...]
    cand = jnp.concatenate([jnp.where(mp == 0, first, other), jnp.where(mp == 0, other, first)], axis=0)

    def compare(val, source):
        product = gram(cand[:, 0:ka], cand[:, 2 * ka:2 * ka + kb], val[:, 0:ka], val[:, 2 * ka:2 * ka + kb])
        product += gram(cand[:, ka:2 * ka], cand[:, 2 * ka + kb:], val[:, ka:2 * ka], val[:, 2 * ka + kb:])
        product = jnp.sum(product.reshape(2 * n_cand, seq, rows_v), axis=1)
        row = lax.broadcasted_iota(jnp.int32, (rows_v, out_own.shape[1]), 0)
        column = lax.broadcasted_iota(jnp.int32, (rows_v, out_own.shape[1]), 1)
        place = column == (2 * source + mp) * n_val + lax.div(row, seq)
        return lax.dot_general(product, place.astype(jnp.float32), (((1,), (0,)), ((), ())),
                               precision=lax.Precision.HIGHEST, preferred_element_type=jnp.float32)

    result = compare(factor_own[rows_c:, :], dp)
    for step in order:
        source = lax.rem(dp - step + n_dp, n_dp)
        remote(factor_val.at[source], factor_val.at[source], f_send.at[source], f_recv.at[source], {"dp": source}).wait_recv()
        result += compare(factor_val[source], source)
    out_own[...] = result
    out_pair = remote(out_own, out_sib, pair_send.at[3], pair_recv.at[3], sibling)
    out_pair.start()
    for copy in f_copies:
        copy.wait_send()
    out_pair.wait()
    scores[...] = out_own[...] + out_sib[...]


def fused(n_dp, cand_x, val_x, cand_grad, val_grad, cand_attn, val_attn, cand_probs, val_probs,
          cand_len, val_len, out_weight, input_proj, grad_proj, attn_proj, value_proj):
    seq, width = cand_x.shape[1:]
    n_cand, n_val = cand_x.shape[0] // 2, val_x.shape[0] // 2
    tokens = (n_cand + n_val) * seq
    rows_c, rows_v = n_cand * seq, n_val * seq
    features = out_weight.shape[1]
    heads = cand_probs.shape[1]
    ka, kb = input_proj.shape[1], grad_proj.shape[1]
    local_kv = value_proj.shape[0] // HEAD_DIM
    bf16, f32 = jnp.bfloat16, jnp.float32
    flat = [part.reshape(-1, part.shape[2]) for part in (cand_x, val_x, cand_grad, val_grad, cand_attn, val_attn)]
    out = jax.ShapeDtypeStruct((2 * n_cand, n_val * 2 * n_dp), f32)
    smem, vmem, hbm = (pl.BlockSpec(memory_space=space) for space in (pltpu.SMEM, pltpu.VMEM, pl.ANY))
    dma = pltpu.SemaphoreType.DMA
    factor = 2 * ka + 2 * kb
    return pl.pallas_call(
        functools.partial(kernel, n_dp),
        out_shape=out,
        in_specs=[smem] * 2 + [hbm] * 9 + [vmem] * 4,
        out_specs=vmem,
        scratch_shapes=[
            pltpu.VMEM((tokens, width), bf16),
            pltpu.VMEM((tokens, width), bf16),
            pltpu.VMEM((2 * tokens, flat[4].shape[1]), bf16),
            pltpu.VMEM(cand_probs.shape, bf16),
            pltpu.VMEM(val_probs.shape, bf16),
            pltpu.VMEM(out_weight.shape, bf16),
            pltpu.VMEM((n_dp, tokens, features), bf16),
            pltpu.VMEM((2, tokens, heads * seq), bf16),
            pltpu.VMEM((tokens, heads * seq), bf16),
            pltpu.VMEM((n_dp, tokens, 2 * heads * seq), bf16),
            pltpu.VMEM((2 * heads * kb, features), bf16),
            pltpu.VMEM((n_cand + n_val, 2 * heads * seq, kb), bf16),
            pltpu.VMEM((2, tokens, ka), f32),
            pltpu.VMEM((tokens, ka), f32),
            pltpu.VMEM((tokens, kb), f32),
            pltpu.VMEM((n_dp, tokens, kb), bf16),
            pltpu.VMEM((n_dp, tokens, kb), bf16),
            pltpu.VMEM((tokens, factor), bf16),
            pltpu.VMEM((rows_c, factor), bf16),
            pltpu.VMEM((n_dp, rows_v, factor), bf16),
            pltpu.VMEM(out.shape, f32),
            pltpu.VMEM(out.shape, f32),
            dma((11,)),
            dma((2, n_dp)), dma((2, n_dp)),
            dma((n_dp,)), dma((n_dp,)), dma((n_dp,)),
            dma((local_kv,)), dma((local_kv,)),
            dma((n_dp,)), dma((n_dp,)), dma((n_dp,)), dma((n_dp,)),
            dma((4,)), dma((4,)),
        ],
        compiler_params=pltpu.CompilerParams(
            collective_id=0, has_side_effects=True, vmem_limit_bytes=60 * 1024 * 1024
        ),
    )(cand_len, val_len, *flat, cand_probs, val_probs, out_weight, input_proj, grad_proj, attn_proj, value_proj)


def solution(mesh):
    placed = (
        P(("grp", "dp"), None, None),
        P(("grp", "dp"), None, None),
        P(("grp", "dp"), None, None),
        P(("grp", "dp"), None, None),
        P(("grp", "dp"), None, "mp"),
        P(("grp", "dp"), None, "mp"),
        P(("grp", "dp"), "mp", None, None),
        P(("grp", "dp"), "mp", None, None),
        P(("grp", "dp")),
        P(("grp", "dp")),
        P("mp", "dp"),
        P(),
        P(),
        P("mp", None),
        P("mp", None),
    )

    n_dp, n_mp = mesh.shape["dp"], mesh.shape["mp"]

    def body(*args):
        features, heads = args[10].shape[1], args[6].shape[1]
        if n_mp == 2 and n_dp % 2 == 0 and features % 128 == 0 and heads % 2 == 0:
            return fused(n_dp, *args)
        return local(n_mp, *args)

    return jax.shard_map(
        body, mesh=mesh, in_specs=placed, out_specs=P(("grp", "dp"), None), check_vma=False
    )
```

```python
import functools

import jax
import jax.numpy as jnp
from jax import lax
from jax.experimental import pallas as pl
from jax.experimental.pallas import tpu as pltpu
from jax.sharding import PartitionSpec as P

HEAD_DIM = 128
EPS = 1e-06


def dot(left, right, contract):
    return lax.dot_general(
        left, right, ((contract[:1], contract[1:]), ((), ())), preferred_element_type=jnp.float32
    )


def gram(left_a, left_b, right_a, right_b):
    return dot(left_a, right_a, (1, 1)) * dot(left_b, right_b, (1, 1))


def own(cand, val, n_mp, index):
    cand_rows, val_rows = cand.shape[0] // n_mp, val.shape[0] // n_mp
    return jnp.concatenate(
        [
            lax.dynamic_slice_in_dim(cand, index * cand_rows, cand_rows, 0),
            lax.dynamic_slice_in_dim(val, index * val_rows, val_rows, 0),
        ],
        axis=0,
    )


def regroup(cand, val, n_mp):
    cand = cand.reshape((n_mp, cand.shape[0] // n_mp) + cand.shape[1:])
    val = val.reshape((n_mp, val.shape[0] // n_mp) + val.shape[1:])
    both = jnp.concatenate([cand, val], axis=1)
    return both.reshape((both.shape[0] * both.shape[1],) + both.shape[2:])


def folded(out_weight, value_proj, local_heads):
    local_kv = value_proj.shape[0] // HEAD_DIM
    group = local_heads // local_kv
    weight = out_weight.reshape(local_kv, group, HEAD_DIM, out_weight.shape[1])
    proj = value_proj.reshape(local_kv, HEAD_DIM, value_proj.shape[1])
    fold = jnp.einsum("kgdf,kdb->fkgb", weight, proj, preferred_element_type=jnp.float32)
    return fold.reshape(out_weight.shape[1], local_heads, -1).astype(jnp.bfloat16)


def local(n_mp, cand_x, val_x, cand_grad, val_grad, cand_attn, val_attn, cand_probs, val_probs,
          cand_len, val_len, out_weight, input_proj, grad_proj, attn_proj, value_proj):
    index = lax.axis_index("mp")
    seq, width = cand_x.shape[1:]
    n_cand = cand_x.shape[0] // n_mp
    count = n_cand + val_x.shape[0] // n_mp
    tokens = count * seq
    heads = cand_probs.shape[1]
    features = out_weight.shape[1]
    n_dp = width // features
    positions = jnp.arange(seq, dtype=jnp.int32)

    grads = own(cand_grad, val_grad, n_mp, index).reshape(tokens, width)
    inputs = own(cand_x, val_x, n_mp, index).reshape(tokens, width)
    length = regroup(cand_len, val_len, n_mp)
    probs = regroup(cand_probs, val_probs, n_mp)
    mask = positions[None, :] < length[:, None]
    probs = jnp.where(mask[:, None, :, None], probs, 0)
    probs = probs.transpose(0, 3, 1, 2).reshape(n_mp * tokens, heads, seq)
    probs = lax.all_to_all(probs, "mp", 0, 1, tiled=True)
    attn = regroup(cand_attn, val_attn, n_mp).reshape(n_mp * tokens, -1)

    spread = lax.all_to_all(grads.reshape(tokens, n_dp, features), "dp", 1, 0, tiled=True)
    spread = spread.reshape(n_dp * count * seq, features)
    probs = lax.all_gather(probs, "dp", axis=0, tiled=True)
    fold = lax.all_gather(folded(out_weight, value_proj, heads), "mp", axis=1, tiled=True)
    all_heads = heads * n_mp
    mixed = dot(spread, fold.reshape(features, -1), (1, 0)).astype(jnp.bfloat16)
    mixed = mixed.reshape(n_dp * count, seq, all_heads, -1)
    probs = probs.reshape(n_dp * count, seq, all_heads, seq)
    b_val = jnp.einsum("ejhi,eihb->ejb", probs, mixed, preferred_element_type=jnp.float32)
    b_val = lax.psum_scatter(b_val, "dp", scatter_dimension=0, tiled=True).reshape(tokens, -1)

    a_in = dot(inputs, input_proj, (1, 0)).astype(jnp.bfloat16)
    live = (positions[None, :] < own(cand_len, val_len, n_mp, index)[:, None]).reshape(tokens, 1)
    b_out = jnp.where(live, dot(grads, grad_proj, (1, 0)), 0.0)
    a_att = dot(attn, attn_proj, (1, 0))
    a_att = lax.psum_scatter(a_att, "mp", scatter_dimension=0, tiled=True).astype(jnp.bfloat16)

    low_out, low_val = b_out.astype(jnp.bfloat16), b_val.astype(jnp.bfloat16)
    square = gram(a_att, low_out, a_att, low_out) + gram(a_in, low_val, a_in, low_val)
    which = jnp.arange(tokens) // seq
    total = jnp.sum(jnp.where(which[:, None] == which[None, :], square, 0.0), axis=1)
    total = jnp.sum(total.reshape(count, seq), axis=1)
    scale = jnp.repeat(lax.rsqrt(jnp.maximum(total, 0.0) + EPS), seq)[:, None]
    factors = jnp.concatenate(
        [a_att, a_in, (b_out * scale).astype(jnp.bfloat16), (b_val * scale).astype(jnp.bfloat16)], axis=1
    )
    rows = n_cand * seq
    ours = factors[:rows]
    theirs = lax.all_gather(factors[rows:], ("dp", "mp"), axis=0, tiled=True)
    ka, kb = a_in.shape[1], b_out.shape[1]
    cuts = (slice(0, ka), slice(2 * ka, 2 * ka + kb), slice(ka, 2 * ka), slice(2 * ka + kb, None))
    first, second, third, fourth = [(ours[:, cut], theirs[:, cut]) for cut in cuts]
    product = gram(first[0], second[0], first[1], second[1]) + gram(third[0], fourth[0], third[1], fourth[1])
    scores = jnp.sum(product.reshape(n_cand, seq, -1, seq), axis=(1, 3))
    return lax.all_gather(scores, "mp", axis=0, tiled=True)


def remote(src, dst, send_sem, recv_sem, device_id):
    return pltpu.make_async_remote_copy(
        src_ref=src, dst_ref=dst, send_sem=send_sem, recv_sem=recv_sem,
        device_id=device_id, device_id_type=pl.DeviceIdType.MESH,
    )


def flipped(index, bits, size):
    other, bit = 0, 1
    while bit < size:
        own_bit = lax.rem(lax.div(index, bit), 2)
        other = other + bit * ((1 - own_bit) if bits & bit else own_bit)
        bit *= 2
    return other


def kernel(
    n_dp,
    cand_len, val_len, cand_x, val_x, cand_grad, val_grad, cand_attn, val_attn, cand_probs, val_probs,
    out_weight, input_proj, grad_proj, attn_proj, value_proj,
    scores,
    g_own, x_own, attn, c_probs, v_probs, weight, g_all, x_half, x_other, x_all, fold, mixed,
    att_send, att_recv, b_own, b_send, b_recv, factor_own, factor_sib, factor_val, out_own, out_sib,
    load_sem, g_send, g_recv, x_send, x_recv, hop_send, fold_send, fold_recv, bs_send, bs_recv,
    f_send, f_recv, pair_send, pair_recv,
):
    dp, mp = lax.axis_index("dp"), lax.axis_index("mp")
    sibling = {"mp": 1 - mp}
    seq = c_probs.shape[2]
    n_cand, n_val = c_probs.shape[0] // 2, v_probs.shape[0] // 2
    count = n_cand + n_val
    rows_c, rows_v = n_cand * seq, n_val * seq
    tokens = rows_c + rows_v
    features = weight.shape[1]
    local_heads = c_probs.shape[1]
    local_kv = value_proj.shape[0] // HEAD_DIM
    group = local_heads // local_kv
    kb = value_proj.shape[1]
    ka = input_proj.shape[0]

    barrier = pltpu.get_barrier_semaphore()
    for step in range(1, n_dp):
        pl.semaphore_signal(barrier, inc=1, device_id={"dp": flipped(dp, step, n_dp)}, device_id_type=pl.DeviceIdType.MESH)
    pl.semaphore_signal(barrier, inc=1, device_id=sibling, device_id_type=pl.DeviceIdType.MESH)

    own_c = pl.ds(pl.multiple_of(mp * rows_c, 16), rows_c)
    own_v = pl.ds(pl.multiple_of(mp * rows_v, 16), rows_v)
    mine = pl.ds(pl.multiple_of(dp * features, 128), features)
    all_c = cand_attn.shape[0]
    loads = []
    pairs = (
        (cand_probs, c_probs), (val_probs, v_probs), (out_weight, weight),
        (cand_grad.at[own_c], g_own.at[pl.ds(0, rows_c)]), (val_grad.at[own_v], g_own.at[pl.ds(rows_c, rows_v)]),
        (cand_attn, attn.at[pl.ds(0, all_c)]), (val_attn, attn.at[pl.ds(all_c, val_attn.shape[0])]),
        (cand_x.at[own_c], x_own.at[pl.ds(0, rows_c)]), (val_x.at[own_v], x_own.at[pl.ds(rows_c, rows_v)]),
        (cand_grad.at[own_c, mine], g_all.at[dp, pl.ds(0, rows_c)]),
        (val_grad.at[own_v, mine], g_all.at[dp, pl.ds(rows_c, rows_v)]),
    )
    for slot, (src, dst) in enumerate(pairs):
        load = pltpu.make_async_copy(src, dst, load_sem.at[slot])
        load.start()
        loads.append(load)
    pl.semaphore_wait(barrier, n_dp)

    near = [2, 1, 3] if n_dp > 2 else [1]
    far = list(range(4, n_dp))
    order = near + far
    spread = sorted(order, key=lambda k: (near.index(k) * len(far) // len(near) + 0.5) if k in near else far.index(k))
    early, late = spread[:4], spread[4:]
    g_copies = []

    def send_tokens(step):
        peer = flipped(dp, step, n_dp)
        theirs = pl.ds(pl.multiple_of(peer * features, 128), features)
        for part, (src, rows, at) in enumerate(((cand_grad, own_c, pl.ds(0, rows_c)), (val_grad, own_v, pl.ds(rows_c, rows_v)))):
            copy = remote(src.at[rows, theirs], g_all.at[dp, at], g_send.at[part, peer], g_recv.at[part, dp], {"dp": peer})
            copy.start()
            g_copies.append(copy)

    for step in early:
        send_tokens(step)

    line, place = n_dp // 2, lax.div(dp, 2)

    def relay_copy(source, direction):
        slot = x_send.at[source] if direction == 1 else x_send.at[n_dp + source]
        return remote(x_all.at[source], x_all.at[source], slot, x_recv.at[source], {"dp": dp + 2 * direction})

    def relay(source, direction):
        @pl.when((place + direction >= 0) & (place + direction < line))
        def _():
            relay_copy(source, direction).start()

    def relay_done(source, direction):
        @pl.when((place + direction >= 0) & (place + direction < line))
        def _():
            relay_copy(source, direction).wait_send()

    def pass_on(source):
        return remote(x_all.at[source], x_all.at[source], hop_send.at[source], x_recv.at[source], partner)

    def at_distance(distance, act):
        for direction in (1, -1):
            @pl.when((place - direction * distance >= 0) & (place - direction * distance < line))
            def _():
                act(dp - 2 * direction * distance, direction)

    def take(source, direction):
        pass_on(source).wait_recv()
        relay(source, direction)
        pass_on(source).start()

    def taken(source, direction):
        relay_done(source, direction)
        pass_on(source).wait_send()

    partner = {"dp": dp + 1 - 2 * lax.rem(dp, 2)}

    loads[0].wait()
    loads[1].wait()
    width = local_heads * seq
    eye = (lax.broadcasted_iota(jnp.int32, (seq, seq), 0) == lax.broadcasted_iota(jnp.int32, (seq, seq), 1)).astype(jnp.bfloat16)
    query = lax.rem(lax.broadcasted_iota(jnp.int32, (seq, width), 1), seq)

    def turn(source, lengths, per_half, offset):
        def body(e, carry):
            flat = source[e].reshape(width, seq)
            turned = dot(eye, flat, (1, 1))
            turned = jnp.where(query < lengths[e], turned, 0.0).astype(jnp.bfloat16)
            at = pl.multiple_of((offset + lax.rem(e, per_half)) * seq, 16)
            x_half[lax.div(e, per_half), pl.ds(at, seq), :] = turned
            return carry
        lax.fori_loop(0, 2 * per_half, body, 0)

    turn(c_probs, cand_len, n_cand, 0)
    turn(v_probs, val_len, n_val, n_cand)
    x_pair = remote(x_half.at[1 - mp], x_other, pair_send.at[0], pair_recv.at[0], sibling)
    x_pair.start()

    loads[2].wait()
    fold_copies = []
    for k in range(local_kv):
        proj = value_proj[k * HEAD_DIM:(k + 1) * HEAD_DIM, :].T
        for h in range(group):
            at = (k * group + h) * HEAD_DIM
            rows = pl.ds(pl.multiple_of((mp * local_heads + k * group + h) * kb, 128), kb)
            fold[rows, :] = dot(proj, weight[at:at + HEAD_DIM, :], (1, 0)).astype(jnp.bfloat16)
        span = pl.ds(pl.multiple_of((mp * local_heads + k * group) * kb, 128), group * kb)
        copy = remote(fold.at[span], fold.at[span], fold_send.at[k], fold_recv.at[k], sibling)
        copy.start()
        fold_copies.append(copy)
        if k == 0:
            x_pair.wait()
            first, other = x_half[mp], x_other[...]
            low, high = jnp.where(mp == 0, first, other), jnp.where(mp == 0, other, first)
            x_all[dp] = jnp.concatenate([low, high], axis=1)
            copy = remote(x_all.at[dp], x_all.at[dp], hop_send.at[dp], x_recv.at[dp], partner)
            copy.start()
            x_copies = [copy]
            for direction in (1, -1):
                relay(dp, direction)
            for step in late:
                send_tokens(step)

    loads[5].wait()
    loads[6].wait()
    for half in range(2):
        att_send[half, pl.ds(0, rows_c), :] = dot(attn[half * rows_c:(half + 1) * rows_c, :], attn_proj[...], (1, 1))
        att_send[half, pl.ds(rows_c, rows_v), :] = dot(
            attn[all_c + half * rows_v:all_c + (half + 1) * rows_v, :], attn_proj[...], (1, 1))
    att_pair = remote(att_send.at[1 - mp], att_recv, pair_send.at[1], pair_recv.at[1], sibling)
    att_pair.start()
    for slot in (3, 4, 7, 8, 9, 10):
        loads[slot].wait()
    a_in = dot(x_own[...], input_proj[...], (1, 1)).astype(jnp.bfloat16)
    b_own[...] = dot(g_own[...], grad_proj[...], (1, 0))
    position = lax.broadcasted_iota(jnp.int32, (seq, kb), 0)
    for e in range(count):
        live = cand_len[mp * n_cand + e] if e < n_cand else val_len[mp * n_val + e - n_cand]
        at = slice(e * seq, (e + 1) * seq)
        b_own[at, :] = jnp.where(position < live, b_own[at, :], 0.0)
    att_pair.wait()
    a_att = (att_send[mp] + att_recv[...]).astype(jnp.bfloat16)
    factor_own[:, 0:2 * ka] = jnp.concatenate([a_att, a_in], axis=1)

    if line > 1:
        at_distance(1, take)
    for k in range(local_kv):
        span = pl.ds(pl.multiple_of(((1 - mp) * local_heads + k * group) * kb, 128), group * kb)
        remote(fold.at[span], fold.at[span], fold_send.at[k], fold_recv.at[k], sibling).wait_recv()

    heads = 2 * local_heads
    batch = 4

    def block(source):
        def heads_step(c, carry):
            rows = pl.ds(pl.multiple_of(c * batch * kb, 128), batch * kb)
            part = dot(g_all[source], fold[rows, :], (1, 1)).astype(jnp.bfloat16)
            for h in range(batch):
                at = pl.ds(pl.multiple_of((c * batch + h) * seq, 16), seq)
                mixed[:, at, :] = part[:, h * kb:(h + 1) * kb].reshape(count, seq, kb)
            return carry
        lax.fori_loop(0, heads // batch, heads_step, 0)

        def prompt_step(e, carry):
            at = pl.ds(pl.multiple_of(e * seq, 16), seq)
            b_send[source, at, :] = dot(x_all[source, at, :], mixed[e], (1, 0)).astype(jnp.bfloat16)
            return carry
        lax.fori_loop(0, count, prompt_step, 0, unroll=4)

    block(dp)
    b_val = b_send[dp].astype(jnp.float32)

    def receive(step, waited):
        source = flipped(dp, step, n_dp)
        for part, at in enumerate((pl.ds(0, rows_c), pl.ds(rows_c, rows_v))):
            remote(g_all.at[source, at], g_all.at[source, at], g_send.at[part, source], g_recv.at[part, source], {"dp": source}).wait_recv()
        if not waited:
            remote(x_all.at[source], x_all.at[source], hop_send.at[source], x_recv.at[source], {"dp": source}).wait_recv()
        block(source)
        copy = remote(b_send.at[source], b_recv.at[dp], bs_send.at[source], bs_recv.at[dp], {"dp": source})
        copy.start()
        return copy

    b_copies, hops = [], 2
    for turn_index, step in enumerate(order):
        if turn_index in (1, 3) and hops < line:
            at_distance(hops, take)
            hops += 1
        if step >= 4:
            while hops < line:
                at_distance(hops, take)
                hops += 1
        b_copies.append(receive(step, step % 2 == 0))
    for step in order:
        source = flipped(dp, step, n_dp)
        remote(b_recv.at[source], b_recv.at[source], bs_send.at[source], bs_recv.at[source], {"dp": source}).wait_recv()
        b_val = b_val + b_recv[source].astype(jnp.float32)

    low_out, low_val = b_own[...].astype(jnp.bfloat16), b_val.astype(jnp.bfloat16)
    square = gram(a_att, low_out, a_att, low_out) + gram(a_in, low_val, a_in, low_val)
    one = lax.div(lax.broadcasted_iota(jnp.int32, (tokens, tokens), 0), seq)
    two = lax.div(lax.broadcasted_iota(jnp.int32, (tokens, tokens), 1), seq)
    same = one == two
    square = jnp.sum(jnp.where(same, square, 0.0), axis=1, keepdims=True)
    square = jnp.broadcast_to(square, (tokens, 128))
    total = lax.dot_general(same.astype(jnp.float32), square, (((1,), (0,)), ((), ())),
                            precision=lax.Precision.HIGHEST, preferred_element_type=jnp.float32)
    scale = lax.rsqrt(jnp.maximum(total[:, 0:1], 0.0) + EPS)
    factor_own[:, 2 * ka:2 * ka + kb] = (b_own[...] * scale).astype(jnp.bfloat16)
    factor_own[:, 2 * ka + kb:] = (b_val * scale).astype(jnp.bfloat16)
    f_copies = []
    val_rows, cand_rows = pl.ds(rows_c, rows_v), pl.ds(0, rows_c)
    for step in order:
        peer = flipped(dp, step, n_dp)
        copy = remote(factor_own.at[val_rows], factor_val.at[dp], f_send.at[peer], f_recv.at[dp], {"dp": peer})
        copy.start()
        f_copies.append(copy)
    f_pair = remote(factor_own.at[cand_rows], factor_sib, pair_send.at[2], pair_recv.at[2], sibling)
    f_pair.start()
    for direction in (1, -1):
        relay_done(dp, direction)
    for distance in range(1, line):
        at_distance(distance, taken)
    for copy in g_copies + x_copies + fold_copies + b_copies:
        copy.wait_send()
    f_pair.wait()

    first, other = factor_own[0:rows_c, :], factor_sib[...]
    cand = jnp.concatenate([jnp.where(mp == 0, first, other), jnp.where(mp == 0, other, first)], axis=0)

    def compare(val, source):
        product = gram(cand[:, 0:ka], cand[:, 2 * ka:2 * ka + kb], val[:, 0:ka], val[:, 2 * ka:2 * ka + kb])
        product += gram(cand[:, ka:2 * ka], cand[:, 2 * ka + kb:], val[:, ka:2 * ka], val[:, 2 * ka + kb:])
        product = jnp.sum(product.reshape(2 * n_cand, seq, rows_v), axis=1)
        row = lax.broadcasted_iota(jnp.int32, (rows_v, out_own.shape[1]), 0)
        column = lax.broadcasted_iota(jnp.int32, (rows_v, out_own.shape[1]), 1)
        place = column == (2 * source + mp) * n_val + lax.div(row, seq)
        return lax.dot_general(product, place.astype(jnp.float32), (((1,), (0,)), ((), ())),
                               precision=lax.Precision.HIGHEST, preferred_element_type=jnp.float32)

    result = compare(factor_own[rows_c:, :], dp)
    for step in order:
        source = flipped(dp, step, n_dp)
        remote(factor_val.at[source], factor_val.at[source], f_send.at[source], f_recv.at[source], {"dp": source}).wait_recv()
        result += compare(factor_val[source], source)
    out_own[...] = result
    out_pair = remote(out_own, out_sib, pair_send.at[3], pair_recv.at[3], sibling)
    out_pair.start()
    for copy in f_copies:
        copy.wait_send()
    out_pair.wait()
    scores[...] = out_own[...] + out_sib[...]


def fused(n_dp, cand_x, val_x, cand_grad, val_grad, cand_attn, val_attn, cand_probs, val_probs,
          cand_len, val_len, out_weight, input_proj, grad_proj, attn_proj, value_proj):
    seq, width = cand_x.shape[1:]
    n_cand, n_val = cand_x.shape[0] // 2, val_x.shape[0] // 2
    tokens = (n_cand + n_val) * seq
    rows_c, rows_v = n_cand * seq, n_val * seq
    features = out_weight.shape[1]
    heads = cand_probs.shape[1]
    ka, kb = input_proj.shape[1], grad_proj.shape[1]
    local_kv = value_proj.shape[0] // HEAD_DIM
    bf16, f32 = jnp.bfloat16, jnp.float32
    flat = [part.reshape(-1, part.shape[2]) for part in (cand_x, val_x, cand_grad, val_grad, cand_attn, val_attn)]
    out = jax.ShapeDtypeStruct((2 * n_cand, n_val * 2 * n_dp), f32)
    smem, vmem, hbm = (pl.BlockSpec(memory_space=space) for space in (pltpu.SMEM, pltpu.VMEM, pl.ANY))
    dma = pltpu.SemaphoreType.DMA
    factor = 2 * ka + 2 * kb
    return pl.pallas_call(
        functools.partial(kernel, n_dp),
        out_shape=out,
        in_specs=[smem] * 2 + [hbm] * 9 + [vmem] * 4,
        out_specs=vmem,
        scratch_shapes=[
            pltpu.VMEM((tokens, width), bf16),
            pltpu.VMEM((tokens, width), bf16),
            pltpu.VMEM((2 * tokens, flat[4].shape[1]), bf16),
            pltpu.VMEM(cand_probs.shape, bf16),
            pltpu.VMEM(val_probs.shape, bf16),
            pltpu.VMEM(out_weight.shape, bf16),
            pltpu.VMEM((n_dp, tokens, features), bf16),
            pltpu.VMEM((2, tokens, heads * seq), bf16),
            pltpu.VMEM((tokens, heads * seq), bf16),
            pltpu.VMEM((n_dp, tokens, 2 * heads * seq), bf16),
            pltpu.VMEM((2 * heads * kb, features), bf16),
            pltpu.VMEM((n_cand + n_val, 2 * heads * seq, kb), bf16),
            pltpu.VMEM((2, tokens, ka), f32),
            pltpu.VMEM((tokens, ka), f32),
            pltpu.VMEM((tokens, kb), f32),
            pltpu.VMEM((n_dp, tokens, kb), bf16),
            pltpu.VMEM((n_dp, tokens, kb), bf16),
            pltpu.VMEM((tokens, factor), bf16),
            pltpu.VMEM((rows_c, factor), bf16),
            pltpu.VMEM((n_dp, rows_v, factor), bf16),
            pltpu.VMEM(out.shape, f32),
            pltpu.VMEM(out.shape, f32),
            dma((11,)),
            dma((2, n_dp)), dma((2, n_dp)),
            dma((2 * n_dp,)), dma((n_dp,)), dma((n_dp,)),
            dma((local_kv,)), dma((local_kv,)),
            dma((n_dp,)), dma((n_dp,)), dma((n_dp,)), dma((n_dp,)),
            dma((4,)), dma((4,)),
        ],
        compiler_params=pltpu.CompilerParams(
            collective_id=0, has_side_effects=True, vmem_limit_bytes=60 * 1024 * 1024
        ),
    )(cand_len, val_len, *flat, cand_probs, val_probs, out_weight, input_proj.T, grad_proj, attn_proj.T, value_proj)


def solution(mesh):
    placed = (
        P(("grp", "dp"), None, None),
        P(("grp", "dp"), None, None),
        P(("grp", "dp"), None, None),
        P(("grp", "dp"), None, None),
        P(("grp", "dp"), None, "mp"),
        P(("grp", "dp"), None, "mp"),
        P(("grp", "dp"), "mp", None, None),
        P(("grp", "dp"), "mp", None, None),
        P(("grp", "dp")),
        P(("grp", "dp")),
        P("mp", "dp"),
        P(),
        P(),
        P("mp", None),
        P("mp", None),
    )

    n_dp, n_mp = mesh.shape["dp"], mesh.shape["mp"]

    def body(*args):
        features, heads = args[10].shape[1], args[6].shape[1]
        if n_mp == 2 and n_dp in (4, 8, 16) and features % 128 == 0 and heads % 2 == 0:
            return fused(n_dp, *args)
        return local(n_mp, *args)

    return jax.shard_map(
        body, mesh=mesh, in_specs=placed, out_specs=P(("grp", "dp"), None), check_vma=False
    )
```

```python
import functools

import jax
import jax.numpy as jnp
from jax import lax
from jax.experimental import pallas as pl
from jax.experimental.pallas import tpu as pltpu
from jax.sharding import PartitionSpec as P

HEAD_DIM = 128
EPS = 1e-06


def dot(left, right, contract):
    return lax.dot_general(
        left, right, ((contract[:1], contract[1:]), ((), ())), preferred_element_type=jnp.float32
    )


def gram(left_a, left_b, right_a, right_b):
    return dot(left_a, right_a, (1, 1)) * dot(left_b, right_b, (1, 1))


def own(cand, val, n_mp, index):
    cand_rows, val_rows = cand.shape[0] // n_mp, val.shape[0] // n_mp
    return jnp.concatenate(
        [
            lax.dynamic_slice_in_dim(cand, index * cand_rows, cand_rows, 0),
            lax.dynamic_slice_in_dim(val, index * val_rows, val_rows, 0),
        ],
        axis=0,
    )


def regroup(cand, val, n_mp):
    cand = cand.reshape((n_mp, cand.shape[0] // n_mp) + cand.shape[1:])
    val = val.reshape((n_mp, val.shape[0] // n_mp) + val.shape[1:])
    both = jnp.concatenate([cand, val], axis=1)
    return both.reshape((both.shape[0] * both.shape[1],) + both.shape[2:])


def folded(out_weight, value_proj, local_heads):
    local_kv = value_proj.shape[0] // HEAD_DIM
    group = local_heads // local_kv
    weight = out_weight.reshape(local_kv, group, HEAD_DIM, out_weight.shape[1])
    proj = value_proj.reshape(local_kv, HEAD_DIM, value_proj.shape[1])
    fold = jnp.einsum("kgdf,kdb->fkgb", weight, proj, preferred_element_type=jnp.float32)
    return fold.reshape(out_weight.shape[1], local_heads, -1).astype(jnp.bfloat16)


def local(n_mp, cand_x, val_x, cand_grad, val_grad, cand_attn, val_attn, cand_probs, val_probs,
          cand_len, val_len, out_weight, input_proj, grad_proj, attn_proj, value_proj):
    index = lax.axis_index("mp")
    seq, width = cand_x.shape[1:]
    n_cand = cand_x.shape[0] // n_mp
    count = n_cand + val_x.shape[0] // n_mp
    tokens = count * seq
    heads = cand_probs.shape[1]
    features = out_weight.shape[1]
    n_dp = width // features
    positions = jnp.arange(seq, dtype=jnp.int32)

    grads = own(cand_grad, val_grad, n_mp, index).reshape(tokens, width)
    inputs = own(cand_x, val_x, n_mp, index).reshape(tokens, width)
    length = regroup(cand_len, val_len, n_mp)
    probs = regroup(cand_probs, val_probs, n_mp)
    mask = positions[None, :] < length[:, None]
    probs = jnp.where(mask[:, None, :, None], probs, 0)
    probs = probs.transpose(0, 3, 1, 2).reshape(n_mp * tokens, heads, seq)
    probs = lax.all_to_all(probs, "mp", 0, 1, tiled=True)
    attn = regroup(cand_attn, val_attn, n_mp).reshape(n_mp * tokens, -1)

    spread = lax.all_to_all(grads.reshape(tokens, n_dp, features), "dp", 1, 0, tiled=True)
    spread = spread.reshape(n_dp * count * seq, features)
    probs = lax.all_gather(probs, "dp", axis=0, tiled=True)
    fold = lax.all_gather(folded(out_weight, value_proj, heads), "mp", axis=1, tiled=True)
    all_heads = heads * n_mp
    mixed = dot(spread, fold.reshape(features, -1), (1, 0)).astype(jnp.bfloat16)
    mixed = mixed.reshape(n_dp * count, seq, all_heads, -1)
    probs = probs.reshape(n_dp * count, seq, all_heads, seq)
    b_val = jnp.einsum("ejhi,eihb->ejb", probs, mixed, preferred_element_type=jnp.float32)
    b_val = lax.psum_scatter(b_val, "dp", scatter_dimension=0, tiled=True).reshape(tokens, -1)

    a_in = dot(inputs, input_proj, (1, 0)).astype(jnp.bfloat16)
    live = (positions[None, :] < own(cand_len, val_len, n_mp, index)[:, None]).reshape(tokens, 1)
    b_out = jnp.where(live, dot(grads, grad_proj, (1, 0)), 0.0)
    a_att = dot(attn, attn_proj, (1, 0))
    a_att = lax.psum_scatter(a_att, "mp", scatter_dimension=0, tiled=True).astype(jnp.bfloat16)

    low_out, low_val = b_out.astype(jnp.bfloat16), b_val.astype(jnp.bfloat16)
    square = gram(a_att, low_out, a_att, low_out) + gram(a_in, low_val, a_in, low_val)
    which = jnp.arange(tokens) // seq
    total = jnp.sum(jnp.where(which[:, None] == which[None, :], square, 0.0), axis=1)
    total = jnp.sum(total.reshape(count, seq), axis=1)
    scale = jnp.repeat(lax.rsqrt(jnp.maximum(total, 0.0) + EPS), seq)[:, None]
    factors = jnp.concatenate(
        [a_att, a_in, (b_out * scale).astype(jnp.bfloat16), (b_val * scale).astype(jnp.bfloat16)], axis=1
    )
    rows = n_cand * seq
    ours = factors[:rows]
    theirs = lax.all_gather(factors[rows:], ("dp", "mp"), axis=0, tiled=True)
    ka, kb = a_in.shape[1], b_out.shape[1]
    cuts = (slice(0, ka), slice(2 * ka, 2 * ka + kb), slice(ka, 2 * ka), slice(2 * ka + kb, None))
    first, second, third, fourth = [(ours[:, cut], theirs[:, cut]) for cut in cuts]
    product = gram(first[0], second[0], first[1], second[1]) + gram(third[0], fourth[0], third[1], fourth[1])
    scores = jnp.sum(product.reshape(n_cand, seq, -1, seq), axis=(1, 3))
    return lax.all_gather(scores, "mp", axis=0, tiled=True)


def remote(src, dst, send_sem, recv_sem, device_id):
    return pltpu.make_async_remote_copy(
        src_ref=src, dst_ref=dst, send_sem=send_sem, recv_sem=recv_sem,
        device_id=device_id, device_id_type=pl.DeviceIdType.MESH,
    )


def flipped(index, bits, size):
    other, bit = 0, 1
    while bit < size:
        own_bit = lax.rem(lax.div(index, bit), 2)
        other = other + bit * ((1 - own_bit) if bits & bit else own_bit)
        bit *= 2
    return other


def kernel(
    n_dp,
    cand_len, val_len, cand_x, val_x, cand_grad, val_grad, cand_attn, val_attn, cand_probs, val_probs,
    out_weight, input_proj, grad_proj, attn_proj, value_proj,
    scores,
    g_own, x_own, attn, c_probs, v_probs, weight, g_all, x_half, x_other, x_all, fold, mixed,
    att_send, att_recv, b_own, b_send, b_recv, factor_own, factor_sib, factor_val, out_own, out_sib,
    load_sem, g_send, g_recv, x_send, x_recv, hop_send, fold_send, fold_recv, bs_send, bs_recv,
    f_send, f_recv, f_hop, pair_send, pair_recv,
):
    dp, mp = lax.axis_index("dp"), lax.axis_index("mp")
    sibling = {"mp": 1 - mp}
    seq = c_probs.shape[2]
    n_cand, n_val = c_probs.shape[0] // 2, v_probs.shape[0] // 2
    count = n_cand + n_val
    rows_c, rows_v = n_cand * seq, n_val * seq
    tokens = rows_c + rows_v
    features = weight.shape[1]
    local_heads = c_probs.shape[1]
    local_kv = value_proj.shape[0] // HEAD_DIM
    group = local_heads // local_kv
    kb = value_proj.shape[1]
    ka = input_proj.shape[0]

    barrier = pltpu.get_barrier_semaphore()
    for step in range(1, n_dp):
        pl.semaphore_signal(barrier, inc=1, device_id={"dp": flipped(dp, step, n_dp)}, device_id_type=pl.DeviceIdType.MESH)
    pl.semaphore_signal(barrier, inc=1, device_id=sibling, device_id_type=pl.DeviceIdType.MESH)

    own_c = pl.ds(pl.multiple_of(mp * rows_c, 16), rows_c)
    own_v = pl.ds(pl.multiple_of(mp * rows_v, 16), rows_v)
    mine = pl.ds(pl.multiple_of(dp * features, 128), features)
    all_c = cand_attn.shape[0]
    loads = []
    pairs = (
        (cand_probs, c_probs), (val_probs, v_probs), (out_weight, weight),
        (cand_grad.at[own_c], g_own.at[pl.ds(0, rows_c)]), (val_grad.at[own_v], g_own.at[pl.ds(rows_c, rows_v)]),
        (cand_attn, attn.at[pl.ds(0, all_c)]), (val_attn, attn.at[pl.ds(all_c, val_attn.shape[0])]),
        (cand_x.at[own_c], x_own.at[pl.ds(0, rows_c)]), (val_x.at[own_v], x_own.at[pl.ds(rows_c, rows_v)]),
        (cand_grad.at[own_c, mine], g_all.at[dp, pl.ds(0, rows_c)]),
        (val_grad.at[own_v, mine], g_all.at[dp, pl.ds(rows_c, rows_v)]),
    )
    for slot, (src, dst) in enumerate(pairs):
        load = pltpu.make_async_copy(src, dst, load_sem.at[slot])
        load.start()
        loads.append(load)
    pl.semaphore_wait(barrier, n_dp)

    near = [2, 1, 3] if n_dp > 2 else [1]
    far = list(range(4, n_dp))
    order = near + far
    spread = sorted(order, key=lambda k: (near.index(k) * len(far) // len(near) + 0.5) if k in near else far.index(k))
    early, late = spread[:4], spread[4:]
    g_copies = []

    def send_tokens(step):
        peer = flipped(dp, step, n_dp)
        theirs = pl.ds(pl.multiple_of(peer * features, 128), features)
        for part, (src, rows, at) in enumerate(((cand_grad, own_c, pl.ds(0, rows_c)), (val_grad, own_v, pl.ds(rows_c, rows_v)))):
            copy = remote(src.at[rows, theirs], g_all.at[dp, at], g_send.at[part, peer], g_recv.at[part, dp], {"dp": peer})
            copy.start()
            g_copies.append(copy)

    for step in early:
        send_tokens(step)

    line, place = n_dp // 2, lax.div(dp, 2)

    def relay_copy(source, direction):
        slot = x_send.at[source] if direction == 1 else x_send.at[n_dp + source]
        return remote(x_all.at[source], x_all.at[source], slot, x_recv.at[source], {"dp": dp + 2 * direction})

    def relay(source, direction):
        @pl.when((place + direction >= 0) & (place + direction < line))
        def _():
            relay_copy(source, direction).start()

    def relay_done(source, direction):
        @pl.when((place + direction >= 0) & (place + direction < line))
        def _():
            relay_copy(source, direction).wait_send()

    def pass_on(source):
        return remote(x_all.at[source], x_all.at[source], hop_send.at[source], x_recv.at[source], partner)

    def at_distance(distance, act):
        for direction in (1, -1):
            @pl.when((place - direction * distance >= 0) & (place - direction * distance < line))
            def _():
                act(dp - 2 * direction * distance, direction)

    def take(source, direction):
        pass_on(source).wait_recv()
        relay(source, direction)
        pass_on(source).start()

    def taken(source, direction):
        relay_done(source, direction)
        pass_on(source).wait_send()

    partner = {"dp": dp + 1 - 2 * lax.rem(dp, 2)}

    loads[0].wait()
    loads[1].wait()
    width = local_heads * seq
    eye = (lax.broadcasted_iota(jnp.int32, (seq, seq), 0) == lax.broadcasted_iota(jnp.int32, (seq, seq), 1)).astype(jnp.bfloat16)
    query = lax.rem(lax.broadcasted_iota(jnp.int32, (seq, width), 1), seq)

    def turn(source, lengths, per_half, offset):
        def body(e, carry):
            flat = source[e].reshape(width, seq)
            turned = dot(eye, flat, (1, 1))
            turned = jnp.where(query < lengths[e], turned, 0.0).astype(jnp.bfloat16)
            at = pl.multiple_of((offset + lax.rem(e, per_half)) * seq, 16)
            x_half[lax.div(e, per_half), pl.ds(at, seq), :] = turned
            return carry
        lax.fori_loop(0, 2 * per_half, body, 0)

    turn(c_probs, cand_len, n_cand, 0)
    turn(v_probs, val_len, n_val, n_cand)
    x_pair = remote(x_half.at[1 - mp], x_other, pair_send.at[0], pair_recv.at[0], sibling)
    x_pair.start()

    loads[2].wait()
    fold_copies = []
    for k in range(local_kv):
        proj = value_proj[k * HEAD_DIM:(k + 1) * HEAD_DIM, :].T
        for h in range(group):
            at = (k * group + h) * HEAD_DIM
            rows = pl.ds(pl.multiple_of((mp * local_heads + k * group + h) * kb, 128), kb)
            fold[rows, :] = dot(proj, weight[at:at + HEAD_DIM, :], (1, 0)).astype(jnp.bfloat16)
        span = pl.ds(pl.multiple_of((mp * local_heads + k * group) * kb, 128), group * kb)
        copy = remote(fold.at[span], fold.at[span], fold_send.at[k], fold_recv.at[k], sibling)
        copy.start()
        fold_copies.append(copy)
        if k == 0:
            x_pair.wait()
            first, other = x_half[mp], x_other[...]
            low, high = jnp.where(mp == 0, first, other), jnp.where(mp == 0, other, first)
            x_all[dp] = jnp.concatenate([low, high], axis=1)
            copy = remote(x_all.at[dp], x_all.at[dp], hop_send.at[dp], x_recv.at[dp], partner)
            copy.start()
            x_copies = [copy]
            for direction in (1, -1):
                relay(dp, direction)
            for step in late:
                send_tokens(step)

    loads[5].wait()
    loads[6].wait()
    for half in range(2):
        att_send[half, pl.ds(0, rows_c), :] = dot(attn[half * rows_c:(half + 1) * rows_c, :], attn_proj[...], (1, 1))
        att_send[half, pl.ds(rows_c, rows_v), :] = dot(
            attn[all_c + half * rows_v:all_c + (half + 1) * rows_v, :], attn_proj[...], (1, 1))
    att_pair = remote(att_send.at[1 - mp], att_recv, pair_send.at[1], pair_recv.at[1], sibling)
    att_pair.start()
    for slot in (3, 4, 7, 8, 9, 10):
        loads[slot].wait()
    a_in = dot(x_own[...], input_proj[...], (1, 1)).astype(jnp.bfloat16)
    b_own[...] = dot(g_own[...], grad_proj[...], (1, 0))
    position = lax.broadcasted_iota(jnp.int32, (seq, kb), 0)
    for e in range(count):
        live = cand_len[mp * n_cand + e] if e < n_cand else val_len[mp * n_val + e - n_cand]
        at = slice(e * seq, (e + 1) * seq)
        b_own[at, :] = jnp.where(position < live, b_own[at, :], 0.0)
    att_pair.wait()
    a_att = (att_send[mp] + att_recv[...]).astype(jnp.bfloat16)
    factor_own[:, 0:2 * ka] = jnp.concatenate([a_att, a_in], axis=1)

    if line > 1:
        at_distance(1, take)
    for k in range(local_kv):
        span = pl.ds(pl.multiple_of(((1 - mp) * local_heads + k * group) * kb, 128), group * kb)
        remote(fold.at[span], fold.at[span], fold_send.at[k], fold_recv.at[k], sibling).wait_recv()

    heads = 2 * local_heads
    batch = 4

    def block(source):
        def heads_step(c, carry):
            rows = pl.ds(pl.multiple_of(c * batch * kb, 128), batch * kb)
            part = dot(g_all[source], fold[rows, :], (1, 1)).astype(jnp.bfloat16)
            for h in range(batch):
                at = pl.ds(pl.multiple_of((c * batch + h) * seq, 16), seq)
                mixed[:, at, :] = part[:, h * kb:(h + 1) * kb].reshape(count, seq, kb)
            return carry
        lax.fori_loop(0, heads // batch, heads_step, 0)

        def prompt_step(e, carry):
            at = pl.ds(pl.multiple_of(e * seq, 16), seq)
            b_send[source, at, :] = dot(x_all[source, at, :], mixed[e], (1, 0)).astype(jnp.bfloat16)
            return carry
        lax.fori_loop(0, count, prompt_step, 0, unroll=4)

    block(dp)
    b_val = b_send[dp].astype(jnp.float32)

    def receive(step, waited):
        source = flipped(dp, step, n_dp)
        for part, at in enumerate((pl.ds(0, rows_c), pl.ds(rows_c, rows_v))):
            remote(g_all.at[source, at], g_all.at[source, at], g_send.at[part, source], g_recv.at[part, source], {"dp": source}).wait_recv()
        if not waited:
            remote(x_all.at[source], x_all.at[source], hop_send.at[source], x_recv.at[source], {"dp": source}).wait_recv()
        block(source)
        copy = remote(b_send.at[source], b_recv.at[dp], bs_send.at[source], bs_recv.at[dp], {"dp": source})
        copy.start()
        return copy

    b_copies, hops = [], 2
    for turn_index, step in enumerate(order):
        if turn_index in (1, 3) and hops < line:
            at_distance(hops, take)
            hops += 1
        if step >= 4:
            while hops < line:
                at_distance(hops, take)
                hops += 1
        b_copies.append(receive(step, step % 2 == 0))
    for step in order:
        source = flipped(dp, step, n_dp)
        remote(b_recv.at[source], b_recv.at[source], bs_send.at[source], bs_recv.at[source], {"dp": source}).wait_recv()
        b_val = b_val + b_recv[source].astype(jnp.float32)

    low_out, low_val = b_own[...].astype(jnp.bfloat16), b_val.astype(jnp.bfloat16)
    square = gram(a_att, low_out, a_att, low_out) + gram(a_in, low_val, a_in, low_val)
    one = lax.div(lax.broadcasted_iota(jnp.int32, (tokens, tokens), 0), seq)
    two = lax.div(lax.broadcasted_iota(jnp.int32, (tokens, tokens), 1), seq)
    same = one == two
    square = jnp.sum(jnp.where(same, square, 0.0), axis=1, keepdims=True)
    square = jnp.broadcast_to(square, (tokens, 128))
    total = lax.dot_general(same.astype(jnp.float32), square, (((1,), (0,)), ((), ())),
                            precision=lax.Precision.HIGHEST, preferred_element_type=jnp.float32)
    scale = lax.rsqrt(jnp.maximum(total[:, 0:1], 0.0) + EPS)
    factor_own[:, 2 * ka:2 * ka + kb] = (b_own[...] * scale).astype(jnp.bfloat16)
    factor_own[:, 2 * ka + kb:] = (b_val * scale).astype(jnp.bfloat16)
    f_copies = []
    cand_rows = pl.ds(0, rows_c)
    factor_val[dp] = factor_own[rows_c:, :]

    def send_factor(source, slot, target):
        copy = remote(factor_val.at[source], factor_val.at[source], slot, f_recv.at[source], target)
        copy.start()
        f_copies.append(copy)

    for step in [k for k in far + near if k % 2 == 0]:
        peer = flipped(dp, step, n_dp)
        send_factor(dp, f_send.at[peer], {"dp": peer})
    send_factor(dp, f_hop.at[dp], partner)
    f_pair = remote(factor_own.at[cand_rows], factor_sib, pair_send.at[2], pair_recv.at[2], sibling)
    f_pair.start()
    def factor_arrives(step):
        source = flipped(dp, step, n_dp)
        remote(factor_val.at[source], factor_val.at[source], f_send.at[source], f_recv.at[source], partner).wait_recv()
        return source

    for step in [k for k in near + far if k % 2 == 0]:
        source = factor_arrives(step)
        send_factor(source, f_hop.at[source], partner)
    f_pair.wait()

    first, other = factor_own[0:rows_c, :], factor_sib[...]
    cand = jnp.concatenate([jnp.where(mp == 0, first, other), jnp.where(mp == 0, other, first)], axis=0)

    for step in [k for k in near + far if k % 2 == 1]:
        factor_arrives(step)
    val = factor_val[...].reshape(n_dp * rows_v, factor_val.shape[2])
    product = gram(cand[:, 0:ka], cand[:, 2 * ka:2 * ka + kb], val[:, 0:ka], val[:, 2 * ka:2 * ka + kb])
    product += gram(cand[:, ka:2 * ka], cand[:, 2 * ka + kb:], val[:, ka:2 * ka], val[:, 2 * ka + kb:])
    product = jnp.sum(product.reshape(2 * n_cand, seq, n_dp * rows_v), axis=1)
    prompt = lax.div(lax.broadcasted_iota(jnp.int32, (n_dp * rows_v, out_own.shape[1]), 0), seq)
    column = lax.broadcasted_iota(jnp.int32, (n_dp * rows_v, out_own.shape[1]), 1)
    chosen = column == (2 * lax.div(prompt, n_val) + mp) * n_val + lax.rem(prompt, n_val)
    out_own[...] = lax.dot_general(product, chosen.astype(jnp.float32), (((1,), (0,)), ((), ())),
                                   precision=lax.Precision.HIGHEST, preferred_element_type=jnp.float32)
    out_pair = remote(out_own, out_sib, pair_send.at[3], pair_recv.at[3], sibling)
    out_pair.start()
    for direction in (1, -1):
        relay_done(dp, direction)
    for distance in range(1, line):
        at_distance(distance, taken)
    for copy in g_copies + x_copies + fold_copies + b_copies:
        copy.wait_send()
    for copy in f_copies:
        copy.wait_send()
    out_pair.wait()
    scores[...] = out_own[...] + out_sib[...]


def fused(n_dp, cand_x, val_x, cand_grad, val_grad, cand_attn, val_attn, cand_probs, val_probs,
          cand_len, val_len, out_weight, input_proj, grad_proj, attn_proj, value_proj):
    seq, width = cand_x.shape[1:]
    n_cand, n_val = cand_x.shape[0] // 2, val_x.shape[0] // 2
    tokens = (n_cand + n_val) * seq
    rows_c, rows_v = n_cand * seq, n_val * seq
    features = out_weight.shape[1]
    heads = cand_probs.shape[1]
    ka, kb = input_proj.shape[1], grad_proj.shape[1]
    local_kv = value_proj.shape[0] // HEAD_DIM
    bf16, f32 = jnp.bfloat16, jnp.float32
    flat = [part.reshape(-1, part.shape[2]) for part in (cand_x, val_x, cand_grad, val_grad, cand_attn, val_attn)]
    out = jax.ShapeDtypeStruct((2 * n_cand, n_val * 2 * n_dp), f32)
    smem, vmem, hbm = (pl.BlockSpec(memory_space=space) for space in (pltpu.SMEM, pltpu.VMEM, pl.ANY))
    dma = pltpu.SemaphoreType.DMA
    factor = 2 * ka + 2 * kb
    return pl.pallas_call(
        functools.partial(kernel, n_dp),
        out_shape=out,
        in_specs=[smem] * 2 + [hbm] * 9 + [vmem] * 4,
        out_specs=vmem,
        scratch_shapes=[
            pltpu.VMEM((tokens, width), bf16),
            pltpu.VMEM((tokens, width), bf16),
            pltpu.VMEM((2 * tokens, flat[4].shape[1]), bf16),
            pltpu.VMEM(cand_probs.shape, bf16),
            pltpu.VMEM(val_probs.shape, bf16),
            pltpu.VMEM(out_weight.shape, bf16),
            pltpu.VMEM((n_dp, tokens, features), bf16),
            pltpu.VMEM((2, tokens, heads * seq), bf16),
            pltpu.VMEM((tokens, heads * seq), bf16),
            pltpu.VMEM((n_dp, tokens, 2 * heads * seq), bf16),
            pltpu.VMEM((2 * heads * kb, features), bf16),
            pltpu.VMEM((n_cand + n_val, 2 * heads * seq, kb), bf16),
            pltpu.VMEM((2, tokens, ka), f32),
            pltpu.VMEM((tokens, ka), f32),
            pltpu.VMEM((tokens, kb), f32),
            pltpu.VMEM((n_dp, tokens, kb), bf16),
            pltpu.VMEM((n_dp, tokens, kb), bf16),
            pltpu.VMEM((tokens, factor), bf16),
            pltpu.VMEM((rows_c, factor), bf16),
            pltpu.VMEM((n_dp, rows_v, factor), bf16),
            pltpu.VMEM(out.shape, f32),
            pltpu.VMEM(out.shape, f32),
            dma((11,)),
            dma((2, n_dp)), dma((2, n_dp)),
            dma((2 * n_dp,)), dma((n_dp,)), dma((n_dp,)),
            dma((local_kv,)), dma((local_kv,)),
            dma((n_dp,)), dma((n_dp,)), dma((n_dp,)), dma((n_dp,)), dma((n_dp,)),
            dma((4,)), dma((4,)),
        ],
        compiler_params=pltpu.CompilerParams(
            collective_id=0, has_side_effects=True, vmem_limit_bytes=60 * 1024 * 1024
        ),
    )(cand_len, val_len, *flat, cand_probs, val_probs, out_weight, input_proj.T, grad_proj, attn_proj.T, value_proj)


def solution(mesh):
    placed = (
        P(("grp", "dp"), None, None),
        P(("grp", "dp"), None, None),
        P(("grp", "dp"), None, None),
        P(("grp", "dp"), None, None),
        P(("grp", "dp"), None, "mp"),
        P(("grp", "dp"), None, "mp"),
        P(("grp", "dp"), "mp", None, None),
        P(("grp", "dp"), "mp", None, None),
        P(("grp", "dp")),
        P(("grp", "dp")),
        P("mp", "dp"),
        P(),
        P(),
        P("mp", None),
        P("mp", None),
    )

    n_dp, n_mp = mesh.shape["dp"], mesh.shape["mp"]

    def body(*args):
        features, heads = args[10].shape[1], args[6].shape[1]
        if n_mp == 2 and n_dp in (4, 8, 16) and features % 128 == 0 and heads % 2 == 0:
            return fused(n_dp, *args)
        return local(n_mp, *args)

    return jax.shard_map(
        body, mesh=mesh, in_specs=placed, out_specs=P(("grp", "dp"), None), check_vma=False
    )
```
